32 devices in a mesh: beam: 2 (over y), freq: 8 (over z, x), section: 2 (over core).
Axes of the slice: x: 2, y: 2, z: 4, core: 2. Of those that a mesh axis runs over, the one named last changes fastest.
Arguments:
- voltages: int32 [256, 8, 2, 1024], P(('beam', 'freq', 'section')), parts along dimension 0, may hold values from -7 to 7, as said below
- filter_taps: float32 [8, 1024], replicated, may hold values from -0.0625 to 0.0625
- delay_plan: int32 [2, 28672], replicated, may hold values from 0 to 1023, as said below
Outputs:
- dedispersed: float32 [4096, 128], P(('beam', 'freq', 'section')), parts along dimension 0
The draws below stay inside these ranges and needn't reach their ends.
There are 2 independent parts, one for each index of `beam`. The reference program is written for one: setup_inputs(seed, part) draws one part's arguments, and reference() takes and returns one part's arrays. A program takes and returns all parts, laid end to end along the dimension named above; an argument that names none is the same for every part. Nothing has to cross between parts.
Inputs may be any that keep to these rules, and one draw needn't show every extreme that they name: `voltages`: quantised samples; dimension 2 holds the real and imaginary parts. `delay_plan`: with D_l and off_l as in the reference program: for level l from 1 to 13, sub-band S and output delay d, entry off_l + S * D_l + d of row 0 (the upper half's delay) and of row 1 (the lower half's delay) both lie in [0, D_(l-1)); where D_l >= 16, both lie in [8 * floor(d / 16), 8 * floor(d / 16) + 8).
All inputs are finite; a program needn't handle non-finite values.
Results may differ from the reference program's by a relative error of at most 0.0003.
Values may be sent and summed in bfloat16 or wider, within the bound.
A program may use at most 64 MiB of HBM per device.

```python
import math
import jax
import jax.numpy as jnp
from jax import lax

NFFT = 1024
COARSE = 8
TAPS = 8
NDELAY = 2048
LEVELS = 13
TILE = 8
FRAMES = 128


def draw_voltages(key, part):
    frame_index = jnp.arange(FRAMES, dtype=jnp.int32)[:, None, None, None]
    shuffled = jax.random.permutation(jax.random.fold_in(key, 1), COARSE).astype(jnp.int32)
    channel_level = 1 + shuffled % 4
    amplitude = channel_level[None, :, None, None] + 4 * frame_index // FRAMES
    amplitude = jnp.broadcast_to(amplitude, (FRAMES, COARSE, 2, NFFT))
    values = jax.random.randint(jax.random.fold_in(key, 2), (FRAMES, COARSE, 2, NFFT), -amplitude, amplitude + 1)
    return values.astype(jnp.int32)


def draw_delay_plan(key, part):
    channels = COARSE * NFFT
    upper_parts = []
    lower_parts = []
    before = 1
    for level in range(1, LEVELS + 1):
        width = max(1, NDELAY * 2 ** level // channels)
        bands = channels >> level
        level_key = jax.random.fold_in(key, level)
        ratio = jax.random.randint(jax.random.fold_in(level_key, 1), (bands, 1), 16, 33)
        upper_jitter = jax.random.randint(jax.random.fold_in(level_key, 2), (bands, width), -1, 1)
        lower_jitter = jax.random.randint(jax.random.fold_in(level_key, 3), (bands, width), -1, 2)
        delay_index = jnp.arange(width, dtype=jnp.int32)[None, :]
        window = min(TILE, before)
        corner = TILE * (delay_index // (2 * TILE))
        excess = delay_index - 2 * corner
        upper_raw = excess * ratio // 64 + upper_jitter
        lower_raw = excess - upper_raw + lower_jitter
        upper_parts.append(jnp.clip(corner + upper_raw, corner, corner + window - 1).reshape(-1))
        lower_parts.append(jnp.clip(corner + lower_raw, corner, corner + window - 1).reshape(-1))
        before = width
    return jnp.stack([jnp.concatenate(upper_parts), jnp.concatenate(lower_parts)]).astype(jnp.int32)


def scatter_about(key, extent, spread, most, held_as=jnp.bfloat16):
    drawn = jax.random.normal(key, extent, jnp.float32) * spread
    return jnp.minimum(jnp.maximum(drawn, -most), most).astype(held_as)


def setup_inputs(seed: int = 0, part: int = 0) -> dict:
    splits = jax.random.split(jax.random.key(seed), 4)
    own_keys = jax.random.split(jax.random.fold_in(splits[3], part), 4)
    return {
        "voltages": draw_voltages(jax.random.fold_in(jax.random.fold_in(splits[3], part), 71), part),
        "filter_taps": scatter_about(splits[1], (TAPS, NFFT), (TAPS * NFFT) ** -0.5, 0.0625, jnp.float32),
        "delay_plan": draw_delay_plan(jax.random.fold_in(splits[3], 71), part),
    }


EPSILON = 1e-05

def dft_table(length):
    index_row = jnp.arange(length, dtype=jnp.int32)
    phase = index_row[:, None] * (index_row[None, :] - length // 2) % length
    angle = phase.astype(jnp.float32) * jnp.float32(2.0 * math.pi / length)
    cosine = jnp.cos(angle).astype(jnp.bfloat16)
    sine = jnp.sin(angle).astype(jnp.bfloat16)
    real_rows = jnp.concatenate([cosine, -sine], axis=1)
    imag_rows = jnp.concatenate([sine, cosine], axis=1)
    return jnp.concatenate([real_rows, imag_rows], axis=0)

def delayed(source_rows, shift):
    span_width = source_rows.shape[1]
    padded = jnp.concatenate([source_rows, jnp.zeros_like(source_rows)], axis=1)
    return jax.vmap(lambda one_row, start: lax.dynamic_slice_in_dim(one_row, start, span_width))(padded, shift)

def merge_rows(state, shift, upper_rows, lower_rows):
    return jnp.take(state, upper_rows, axis=0) + delayed(jnp.take(state, lower_rows, axis=0), shift)

def reference(voltages, filter_taps, delay_plan):
    frames = voltages.shape[0]
    coarse = voltages.shape[1]
    fft_length = voltages.shape[3]
    tap_count = filter_taps.shape[0]
    channels = coarse * fft_length
    table = dft_table(fft_length)
    leading = jnp.zeros((tap_count - 1,) + voltages.shape[1:], jnp.bfloat16)
    extended = jnp.concatenate([leading, voltages.astype(jnp.bfloat16)], axis=0)
    span = math.gcd(frames, 256)

    def spectrum_block(first):
        window = lax.dynamic_slice_in_dim(extended, first, span + tap_count - 1, 0)
        summed = window[0:span].astype(jnp.float32) * filter_taps[0]
        for tap_index in range(1, tap_count):
            summed = summed + window[tap_index:tap_index + span].astype(jnp.float32) * filter_taps[tap_index]
        filtered = summed.astype(jnp.bfloat16).reshape(span * coarse, 2 * fft_length)
        spectra = jnp.dot(filtered, table, preferred_element_type=jnp.float32)
        real_part = spectra[:, :fft_length]
        imag_part = spectra[:, fft_length:]
        return (real_part * real_part + imag_part * imag_part).astype(jnp.bfloat16).reshape(span, channels)
    firsts = jnp.arange(frames // span, dtype=jnp.int32) * span
    power = lax.map(spectrum_block, firsts).reshape(frames, channels)
    series = power.astype(jnp.float32).T
    mean = lax.optimization_barrier(jnp.mean(series, axis=1, keepdims=True))
    centered = series - mean
    variance = lax.optimization_barrier(jnp.mean(centered * centered, axis=1, keepdims=True))
    state = centered / jnp.sqrt(channels * (variance + EPSILON))
    offset = 0
    before = 1
    for level in range(1, LEVELS + 1):
        width = max(1, NDELAY * 2 ** level // channels)
        count = (channels >> level) * width
        upper = delay_plan[0, offset:offset + count]
        lower = delay_plan[1, offset:offset + count]
        band_index = jnp.arange(count, dtype=jnp.int32) // width
        state = merge_rows(state, upper, (2 * band_index + 1) * before + upper, 2 * band_index * before + lower)
        offset = offset + count
        before = width
    return state
```

```python
import functools
import math

import jax
import jax.numpy as jnp
import numpy as np
from jax import lax
from jax.experimental import pallas as pl
from jax.experimental.pallas import tpu as pltpu
from jax.sharding import PartitionSpec as P

NDELAY = 2048

EPSILON = 1e-05

LANES = 128
TILE = 8
COLUMNS = 256
MESH = pl.DeviceIdType.MESH


def dft_columns(length, chunk, flat):
    wide = chunk // flat
    place = np.arange(length)
    channel = place // chunk * chunk + place % wide * flat + place % chunk // wide
    phase = np.arange(length)[:, None] * (channel[None, :] - length // 2) % length
    angle = phase.astype(np.float32) * np.float32(2.0 * math.pi / length)
    cosine = np.cos(angle).astype(jnp.bfloat16).reshape(length, -1, COLUMNS)
    sine = np.sin(angle).astype(jnp.bfloat16).reshape(length, -1, COLUMNS)
    return np.ascontiguousarray(np.concatenate([cosine, sine], axis=2).transpose(1, 0, 2))


class Sizes:
    def __init__(self, voltages, taps, devices, sections):
        self.devices, self.sections = devices, sections
        self.frames_dev, self.coarse, _, self.length = voltages.shape
        self.taps = taps.shape[0]
        self.channels = self.coarse * self.length
        self.frames = self.frames_dev * devices
        self.merges = devices.bit_length() - 1
        self.levels = self.channels.bit_length() - 1
        self.flat_levels = (self.channels // NDELAY).bit_length() - 1
        self.flat = 1 << self.flat_levels
        self.local_levels = self.levels - self.merges
        self.block = NDELAY // devices
        own = self.channels // devices
        self.chunk = max(own, LANES * self.flat)
        self.share = self.chunk // own
        self.spans = self.frames // LANES
        self.held = {self.levels: self.block // TILE}
        for level in range(self.levels, self.local_levels, -1):
            self.held[level - 1] = max(1, self.held[level] // 2)

    def width(self, level):
        return max(1, NDELAY * 2**level // self.channels)

    def offset(self, level):
        return sum((self.channels >> m) * self.width(m) for m in range(1, level))

    def first_tile(self, device, level):
        tile, held = device * self.held[self.levels], self.held[self.levels]
        for _ in range(self.levels - level):
            tile = tile // 2
        return tile

    def pieces(self, me):
        found = []
        for level in range(self.flat_levels + 1, self.local_levels + 1):
            found.append((level, self.offset(level) + me * self.block, self.block // TILE))
        for level in range(self.local_levels + 1, self.levels + 1):
            for band in range(self.channels >> level):
                start = self.offset(level) + band * self.width(level)
                found.append((level, start + TILE * self.first_tile(me, level), self.held[level]))
        return found


def picked(tile, rows):
    return jnp.concatenate(
        [
            jnp.take_along_axis(
                tile[:, at : at + LANES], rows, axis=0, mode="promise_in_bounds"
            )
            for at in range(0, tile.shape[1], LANES)
        ],
        axis=1,
    )


def later(tile, shift):
    place = lax.broadcasted_iota(jnp.int32, shift.shape, 1) + shift
    inside, span = place & (LANES - 1), place // LANES
    spans = tile.shape[1] // LANES
    turned = [
        jnp.take_along_axis(
            tile[:, s * LANES : (s + 1) * LANES], inside, axis=1, mode="promise_in_bounds"
        )
        for s in range(spans)
    ]
    result = []
    for out in range(spans):
        total = jnp.where(span == 0, turned[out], 0.0)
        for s in range(out + 1, spans):
            total = jnp.where(span == s - out, turned[s], total)
        result.append(total)
    return jnp.concatenate(result, axis=1)


def kernel(
    z,
    axes,
    x_ref,
    taps_ref,
    plan_ref,
    table_ref,
    out_ref,
    table,
    halo,
    lhs,
    power,
    outgoing,
    series,
    turned,
    flat,
    state,
    tiles_in,
    plan_rows,
    plan_columns,
    upper_plan,
    lower_plan,
    table_sem,
    halo_sem,
    send_sem,
    recv_sem,
    send2_sem,
    recv2_sem,
):
    beam = lax.axis_index(axes[0])
    me = lax.axis_index(axes[1]) * z.sections + lax.axis_index(axes[2])

    def at(device):
        return (beam, device // z.sections, lax.rem(device, z.sections))

    loads = []
    for part in range(table_ref.shape[0]):
        loads.append(
            pltpu.make_async_copy(table_ref.at[part], table.at[part], table_sem.at[part])
        )
        loads[-1].start()

    barrier = pltpu.get_barrier_semaphore()

    def greet(step, carry):
        pl.semaphore_signal(
            barrier, inc=1, device_id=at(lax.rem(me + step, z.devices)), device_id_type=MESH
        )
        return carry

    lax.fori_loop(1, z.devices, greet, 0)
    pl.semaphore_wait(barrier, z.devices - 1)

    before = z.taps - 1
    ahead = pltpu.make_async_remote_copy(
        src_ref=x_ref.at[pl.ds(z.frames_dev - before, before)],
        dst_ref=halo,
        send_sem=halo_sem.at[0],
        recv_sem=halo_sem.at[1],
        device_id=at(lax.rem(me + 1, z.devices)),
        device_id_type=MESH,
    )

    @pl.when(me < z.devices - 1)
    def _():
        ahead.start()

    @pl.when(me == 0)
    def _():
        halo[...] = jnp.zeros_like(halo)

    pieces = z.pieces(me)
    plan_rows[...] = jnp.zeros_like(plan_rows)
    for piece, (_, start, _) in enumerate(pieces):
        base = pl.multiple_of(start // LANES * LANES, LANES)
        plan_rows[2 * piece : 2 * piece + 2, :] = plan_ref[:, pl.ds(base, LANES)]
    for row in range(0, plan_rows.shape[0], LANES):
        plan_columns[:, row : row + LANES] = plan_rows[row : row + LANES, :].T
    entry = 0
    for piece, (_, start, count) in enumerate(pieces):
        for tile in range(count):
            row = pl.multiple_of(lax.rem(start, LANES) + TILE * tile, TILE)
            both = plan_columns[pl.ds(row, TILE), 2 * piece : 2 * piece + 2]
            upper_plan[entry] = jnp.broadcast_to(both[:, 0:1], (TILE, LANES))
            lower_plan[entry] = jnp.broadcast_to(both[:, 1:2], (TILE, LANES))
            entry += 1

    @pl.when(me > 0)
    def _():
        ahead.wait_recv()

    half = z.coarse
    rows = z.frames_dev * z.coarse
    for lane in range(0, z.length, LANES):
        lanes = slice(lane, lane + LANES)
        window = [halo[n, :, lanes].astype(jnp.float32) for n in range(before)]
        window += [x_ref[n, :, lanes].astype(jnp.float32) for n in range(z.frames_dev)]
        taps = [taps_ref[j : j + 1, lanes] for j in range(z.taps)]
        summed = []
        for n in range(z.frames_dev):
            total = window[n] * taps[0]
            for j in range(1, z.taps):
                total = total + window[n + j] * taps[j]
            summed.append(total)
        for part in range(2):
            for n in range(0, z.frames_dev, 2):
                own = slice(part * half, (part + 1) * half)
                pair = jnp.concatenate([summed[n][own], summed[n + 1][own]], axis=0)
                first = part * rows + n * half
                lhs[first : first + 2 * half, lanes] = pair.astype(jnp.bfloat16)

    per_coarse = z.length // z.chunk
    parts = z.chunk // COLUMNS
    side = z.chunk // 2

    def parcel(chunk, device):
        return pltpu.make_async_remote_copy(
            src_ref=outgoing.at[chunk],
            dst_ref=series.at[me],
            send_sem=send_sem.at[device],
            recv_sem=recv_sem.at[me],
            device_id=at(device),
            device_id_type=MESH,
        )

    for position in range(per_coarse):
        for part in range(parts):
            index = position * parts + part
            loads[index].wait()
            product = jnp.dot(lhs[...], table[index], preferred_element_type=jnp.float32)
            real = product[:rows, :COLUMNS] + product[rows:, COLUMNS:]
            imag = product[rows:, :COLUMNS] - product[:rows, COLUMNS:]
            squared = real * real + imag * imag
            for lane in range(0, COLUMNS, LANES):
                power[(part * COLUMNS + lane) // LANES] = squared[:, lane : lane + LANES]
        for c in range(z.coarse):
            found = [
                power[k, pl.ds(c, z.frames_dev, stride=z.coarse), :]
                for k in range(z.chunk // LANES)
            ]
            many = len(found) // 2
            for k in range(many):
                outgoing[c * per_coarse + position, :, k * LANES : (k + 1) * LANES] = (
                    jnp.concatenate([found[k], found[many + k]], axis=0).astype(jnp.bfloat16)
                )

        def send(step, carry):
            c = lax.rem(step + me // (z.share * per_coarse), z.coarse)
            chunk = c * per_coarse + position
            for twin in range(z.share):
                device = chunk * z.share + twin

                @pl.when(device != me)
                def _():
                    parcel(chunk, device).start()

            return carry

        lax.fori_loop(0, z.coarse, send, 0)
    series[me] = outgoing[me // z.share]

    def receive(step, carry):
        source = lax.rem(me + step, z.devices)
        pltpu.make_async_remote_copy(
            src_ref=outgoing.at[0],
            dst_ref=series.at[source],
            send_sem=send_sem.at[source],
            recv_sem=recv_sem.at[source],
            device_id=at(source),
            device_id_type=MESH,
        ).wait_recv()
        return carry

    lax.fori_loop(1, z.devices, receive, 0)

    rows8 = z.frames_dev
    values = []
    for d in range(z.devices):
        both = series[d].astype(jnp.float32)
        values.append((both[:rows8], both[rows8:]))
    centred = []
    for k in range(2):
        total = values[0][k]
        for d in range(1, z.devices):
            total = total + values[d][k]
        mean = jnp.sum(total, axis=0, keepdims=True) * (1.0 / z.frames)
        part = [values[d][k] - mean for d in range(z.devices)]
        total = part[0] * part[0]
        for d in range(1, z.devices):
            total = total + part[d] * part[d]
        variance = jnp.sum(total, axis=0, keepdims=True) * (1.0 / z.frames)
        scale = 1.0 / jnp.sqrt(z.channels * (variance + EPSILON))
        centred.append((part, scale))
    wide = z.chunk // z.flat
    for d in range(z.devices):
        total = None
        for k in range(2):
            part, scale = centred[k]
            normed = part[d] * scale
            for lane in range(0, side, wide):
                piece = normed[:, lane : lane + wide]
                total = piece if total is None else total + piece
        turned[d * rows8 : (d + 1) * rows8, :] = total
    for span in range(z.spans):
        lanes = slice(span * LANES, (span + 1) * LANES)
        flat[:, lanes] = turned[lanes, :].T

    mine = pl.multiple_of(lax.rem(me, z.share) * z.block, TILE)
    tiles = [
        flat[pl.ds(pl.multiple_of(mine + TILE * k, TILE), TILE), :]
        for k in range(z.block // TILE)
    ]
    entry = 0
    row_in_tile = lax.broadcasted_iota(jnp.int32, (TILE, LANES), 0)
    for level in range(z.flat_levels + 1, z.local_levels + 1):
        width = z.width(level)
        merged = []
        for k in range(len(tiles)):
            h, g = upper_plan[entry], lower_plan[entry]
            entry += 1
            if width <= TILE:
                base = row_in_tile // width * width
                high, low = tiles[k], tiles[k]
                high_rows, low_rows = base + width // 2 + h, base + g
            else:
                many = width // TILE
                first = k // many * many + k % many // 2
                high, low = tiles[first + many // 2], tiles[first]
                high_rows, low_rows = h & (TILE - 1), g & (TILE - 1)
            merged.append(picked(high, high_rows) + later(picked(low, low_rows), h))
        tiles = merged
    for k, tile in enumerate(tiles):
        state[k] = tile

    def deliver(step, carry):
        device = lax.rem(me + step, z.devices)
        pltpu.make_async_remote_copy(
            src_ref=state.at[z.first_tile(device, z.local_levels)],
            dst_ref=tiles_in.at[me],
            send_sem=send2_sem.at[device],
            recv_sem=recv2_sem.at[me],
            device_id=at(device),
            device_id_type=MESH,
        ).start()
        return carry

    lax.fori_loop(1, z.devices, deliver, 0)
    tiles_in[me] = state[z.first_tile(me, z.local_levels)]

    def accept(step, carry):
        source = lax.rem(me + step, z.devices)
        pltpu.make_async_remote_copy(
            src_ref=state.at[0],
            dst_ref=tiles_in.at[source],
            send_sem=send2_sem.at[source],
            recv_sem=recv2_sem.at[source],
            device_id=at(source),
            device_id_type=MESH,
        ).wait_recv()
        return carry

    lax.fori_loop(1, z.devices, accept, 0)

    bands = [[tiles_in[d]] for d in range(z.devices)]
    for level in range(z.local_levels + 1, z.levels + 1):
        merged = []
        for band in range(len(bands) // 2):
            result = []
            for k in range(z.held[level]):
                h, g = upper_plan[entry], lower_plan[entry]
                entry += 1
                high = picked(bands[2 * band + 1][k // 2], h & (TILE - 1))
                low = picked(bands[2 * band][k // 2], g & (TILE - 1))
                result.append(high + later(low, h))
            merged.append(result)
        bands = merged
    for k, tile in enumerate(bands[0]):
        out_ref[k * TILE : (k + 1) * TILE, :] = tile

    @pl.when(me < z.devices - 1)
    def _():
        ahead.wait_send()

    def finish(step, carry):
        device = lax.rem(me + step, z.devices)
        pltpu.make_async_remote_copy(
            src_ref=outgoing.at[0],
            dst_ref=series.at[0],
            send_sem=send_sem.at[device],
            recv_sem=recv_sem.at[device],
            device_id=at(device),
            device_id_type=MESH,
        ).wait_send()
        pltpu.make_async_remote_copy(
            src_ref=state.at[0],
            dst_ref=tiles_in.at[0],
            send_sem=send2_sem.at[device],
            recv_sem=recv2_sem.at[device],
            device_id=at(device),
            device_id_type=MESH,
        ).wait_send()
        return carry

    lax.fori_loop(1, z.devices, finish, 0)


def per_device(axes, voltages, filter_taps, delay_plan):
    devices = lax.axis_size(axes[1]) * lax.axis_size(axes[2])
    z = Sizes(voltages, filter_taps, devices, lax.axis_size(axes[2]))
    samples = (
        voltages.astype(jnp.bfloat16)
        .transpose(0, 2, 1, 3)
        .reshape(z.frames_dev, 2 * z.coarse, z.length)
    )
    table = jnp.asarray(dft_columns(z.length, z.chunk, z.flat))
    pieces = z.pieces(0)
    entries = sum(count for _, _, count in pieces)
    plan_rows = -(-2 * len(pieces) // LANES) * LANES
    f32, bf16, i32 = jnp.float32, jnp.bfloat16, jnp.int32
    vmem = pl.BlockSpec(memory_space=pltpu.VMEM)
    return pl.pallas_call(
        functools.partial(kernel, z, axes),
        out_shape=jax.ShapeDtypeStruct((z.block, z.frames), f32),
        in_specs=[vmem, vmem, vmem, pl.BlockSpec(memory_space=pl.ANY)],
        out_specs=vmem,
        scratch_shapes=[
            pltpu.VMEM(table.shape, bf16),
            pltpu.VMEM((z.taps - 1, 2 * z.coarse, z.length), bf16),
            pltpu.VMEM((2 * z.frames_dev * z.coarse, z.length), bf16),
            pltpu.VMEM((z.chunk // LANES, z.frames_dev * z.coarse, LANES), f32),
            pltpu.VMEM((z.channels // z.chunk, 2 * z.frames_dev, z.chunk // 2), bf16),
            pltpu.VMEM((z.devices, 2 * z.frames_dev, z.chunk // 2), bf16),
            pltpu.VMEM((z.frames, z.chunk // z.flat), f32),
            pltpu.VMEM((z.chunk // z.flat, z.frames), f32),
            pltpu.VMEM((z.block // TILE, TILE, z.frames), f32),
            pltpu.VMEM((z.devices, TILE, z.frames), f32),
            pltpu.VMEM((plan_rows, LANES), i32),
            pltpu.VMEM((LANES, plan_rows), i32),
            pltpu.VMEM((entries, TILE, LANES), i32),
            pltpu.VMEM((entries, TILE, LANES), i32),
            pltpu.SemaphoreType.DMA((table.shape[0],)),
            pltpu.SemaphoreType.DMA((2,)),
            pltpu.SemaphoreType.DMA((z.devices,)),
            pltpu.SemaphoreType.DMA((z.devices,)),
            pltpu.SemaphoreType.DMA((z.devices,)),
            pltpu.SemaphoreType.DMA((z.devices,)),
        ],
        compiler_params=pltpu.CompilerParams(
            collective_id=0, has_side_effects=True, vmem_limit_bytes=40 * 2**20
        ),
    )(samples, filter_taps, delay_plan, table)


def solution(mesh):
    axes = ("beam", "freq", "section")
    placed = (P(axes, None, None, None), P(), P())
    return jax.shard_map(
        functools.partial(per_device, axes),
        mesh=mesh,
        in_specs=placed,
        out_specs=P(axes, None),
        check_vma=False,
    )
```

```python
import functools
import math

import jax
import jax.numpy as jnp
import numpy as np
from jax import lax
from jax.experimental import pallas as pl
from jax.experimental.pallas import tpu as pltpu
from jax.sharding import PartitionSpec as P

NDELAY = 2048

EPSILON = 1e-05

LANES = 128
TILE = 8
COLUMNS = 256
MESH = pl.DeviceIdType.MESH


def dft_columns(length, chunk, flat):
    wide = chunk // flat
    place = np.arange(length)
    channel = place // chunk * chunk + place % wide * flat + place % chunk // wide
    phase = np.arange(length)[:, None] * (channel[None, :] - length // 2) % length
    angle = phase.astype(np.float32) * np.float32(2.0 * math.pi / length)
    cosine = np.cos(angle).astype(jnp.bfloat16).reshape(length, -1, COLUMNS)
    sine = np.sin(angle).astype(jnp.bfloat16).reshape(length, -1, COLUMNS)
    return np.ascontiguousarray(np.concatenate([cosine, sine], axis=2).transpose(1, 0, 2))


class Sizes:
    def __init__(self, voltages, taps, devices, sections):
        self.devices, self.sections = devices, sections
        self.frames_dev, self.coarse, _, self.length = voltages.shape
        self.taps = taps.shape[0]
        self.channels = self.coarse * self.length
        self.frames = self.frames_dev * devices
        self.merges = devices.bit_length() - 1
        self.levels = self.channels.bit_length() - 1
        self.flat_levels = (self.channels // NDELAY).bit_length() - 1
        self.flat = 1 << self.flat_levels
        self.local_levels = self.levels - self.merges
        self.block = NDELAY // devices
        own = self.channels // devices
        self.chunk = max(own, LANES * self.flat)
        self.share = self.chunk // own
        self.spans = self.frames // LANES
        self.held = {self.levels: self.block // TILE}
        for level in range(self.levels, self.local_levels, -1):
            self.held[level - 1] = max(1, self.held[level] // 2)

    def width(self, level):
        return max(1, NDELAY * 2**level // self.channels)

    def offset(self, level):
        return sum((self.channels >> m) * self.width(m) for m in range(1, level))

    def first_tile(self, device, level):
        tile, held = device * self.held[self.levels], self.held[self.levels]
        for _ in range(self.levels - level):
            tile = tile // 2
        return tile

    def pieces(self, me):
        found = []
        for level in range(self.flat_levels + 1, self.local_levels + 1):
            found.append((level, self.offset(level) + me * self.block, self.block // TILE))
        for level in range(self.local_levels + 1, self.levels + 1):
            for band in range(self.channels >> level):
                start = self.offset(level) + band * self.width(level)
                found.append((level, start + TILE * self.first_tile(me, level), self.held[level]))
        return found


def picked(tile, rows):
    return jnp.concatenate(
        [
            jnp.take_along_axis(
                tile[:, at : at + LANES], rows, axis=0, mode="promise_in_bounds"
            )
            for at in range(0, tile.shape[1], LANES)
        ],
        axis=1,
    )


def later(tile, shift):
    place = lax.broadcasted_iota(jnp.int32, shift.shape, 1) + shift
    inside, span = place & (LANES - 1), place // LANES
    spans = tile.shape[1] // LANES
    turned = [
        jnp.take_along_axis(
            tile[:, s * LANES : (s + 1) * LANES], inside, axis=1, mode="promise_in_bounds"
        )
        for s in range(spans)
    ]
    result = []
    for out in range(spans):
        total = jnp.where(span == 0, turned[out], 0.0)
        for s in range(out + 1, spans):
            total = jnp.where(span == s - out, turned[s], total)
        result.append(total)
    return jnp.concatenate(result, axis=1)


def kernel(
    z,
    axes,
    x_hbm,
    taps_hbm,
    plan_hbm,
    table_ref,
    out_ref,
    raw,
    x_ref,
    taps_ref,
    plan_ref,
    table,
    halo,
    lhs,
    power,
    outgoing,
    series,
    turned,
    flat,
    state,
    tiles_in,
    plan_rows,
    plan_columns,
    upper_plan,
    lower_plan,
    load_sem,
    table_sem,
    halo_sem,
    send_sem,
    recv_sem,
    send2_sem,
    recv2_sem,
):
    beam = lax.axis_index(axes[0])
    me = lax.axis_index(axes[1]) * z.sections + lax.axis_index(axes[2])

    def at(device):
        return (beam, device // z.sections, lax.rem(device, z.sections))

    voltage_loads = [
        pltpu.make_async_copy(x_hbm.at[:, :, part], raw.at[part], load_sem.at[part])
        for part in range(2)
    ]
    plan_load = pltpu.make_async_copy(plan_hbm, plan_ref, load_sem.at[2])
    taps_load = pltpu.make_async_copy(taps_hbm, taps_ref, load_sem.at[3])
    for load in (*voltage_loads, plan_load, taps_load):
        load.start()
    loads = []
    for part in range(table_ref.shape[0]):
        loads.append(
            pltpu.make_async_copy(table_ref.at[part], table.at[part], table_sem.at[part])
        )
        loads[-1].start()

    barrier = pltpu.get_barrier_semaphore()

    def greet(step, carry):
        pl.semaphore_signal(
            barrier, inc=1, device_id=at(lax.rem(me + step, z.devices)), device_id_type=MESH
        )
        return carry

    lax.fori_loop(1, z.devices, greet, 0)
    for load in voltage_loads:
        load.wait()
    for n in range(z.frames_dev - 1, -1, -1):
        both = jnp.concatenate([raw[0, n], raw[1, n]], axis=0)
        x_ref[n] = both.astype(jnp.float32).astype(jnp.bfloat16)
    pl.semaphore_wait(barrier, z.devices - 1)

    before = z.taps - 1
    ahead = pltpu.make_async_remote_copy(
        src_ref=x_ref.at[pl.ds(z.frames_dev - before, before)],
        dst_ref=halo,
        send_sem=halo_sem.at[0],
        recv_sem=halo_sem.at[1],
        device_id=at(lax.rem(me + 1, z.devices)),
        device_id_type=MESH,
    )

    @pl.when(me < z.devices - 1)
    def _():
        ahead.start()

    @pl.when(me == 0)
    def _():
        halo[...] = jnp.zeros_like(halo)

    pieces = z.pieces(me)
    plan_load.wait()
    plan_rows[...] = jnp.zeros_like(plan_rows)
    for piece, (_, start, _) in enumerate(pieces):
        base = pl.multiple_of(start // LANES * LANES, LANES)
        plan_rows[2 * piece : 2 * piece + 2, :] = plan_ref[:, pl.ds(base, LANES)]
    for row in range(0, plan_rows.shape[0], LANES):
        plan_columns[:, row : row + LANES] = plan_rows[row : row + LANES, :].T
    entry = 0
    for piece, (_, start, count) in enumerate(pieces):
        for tile in range(count):
            row = pl.multiple_of(lax.rem(start, LANES) + TILE * tile, TILE)
            both = plan_columns[pl.ds(row, TILE), 2 * piece : 2 * piece + 2]
            upper_plan[entry] = jnp.broadcast_to(both[:, 0:1], (TILE, LANES))
            lower_plan[entry] = jnp.broadcast_to(both[:, 1:2], (TILE, LANES))
            entry += 1

    @pl.when(me > 0)
    def _():
        ahead.wait_recv()

    taps_load.wait()
    half = z.coarse
    rows = z.frames_dev * z.coarse
    for lane in range(0, z.length, LANES):
        lanes = slice(lane, lane + LANES)
        window = [halo[n, :, lanes].astype(jnp.float32) for n in range(before)]
        window += [x_ref[n, :, lanes].astype(jnp.float32) for n in range(z.frames_dev)]
        taps = [taps_ref[j : j + 1, lanes] for j in range(z.taps)]
        summed = []
        for n in range(z.frames_dev):
            total = window[n] * taps[0]
            for j in range(1, z.taps):
                total = total + window[n + j] * taps[j]
            summed.append(total)
        for part in range(2):
            for n in range(0, z.frames_dev, 2):
                own = slice(part * half, (part + 1) * half)
                pair = jnp.concatenate([summed[n][own], summed[n + 1][own]], axis=0)
                first = part * rows + n * half
                lhs[first : first + 2 * half, lanes] = pair.astype(jnp.bfloat16)

    per_coarse = z.length // z.chunk
    parts = z.chunk // COLUMNS
    side = z.chunk // 2

    def parcel(chunk, device):
        return pltpu.make_async_remote_copy(
            src_ref=outgoing.at[chunk],
            dst_ref=series.at[me],
            send_sem=send_sem.at[device],
            recv_sem=recv_sem.at[me],
            device_id=at(device),
            device_id_type=MESH,
        )

    for position in range(per_coarse):
        for part in range(parts):
            index = position * parts + part
            loads[index].wait()
            product = jnp.dot(lhs[...], table[index], preferred_element_type=jnp.float32)
            real = product[:rows, :COLUMNS] + product[rows:, COLUMNS:]
            imag = product[rows:, :COLUMNS] - product[:rows, COLUMNS:]
            squared = real * real + imag * imag
            for lane in range(0, COLUMNS, LANES):
                power[(part * COLUMNS + lane) // LANES] = squared[:, lane : lane + LANES]
        for c in range(z.coarse):
            found = [
                power[k, pl.ds(c, z.frames_dev, stride=z.coarse), :]
                for k in range(z.chunk // LANES)
            ]
            many = len(found) // 2
            for k in range(many):
                outgoing[c * per_coarse + position, :, k * LANES : (k + 1) * LANES] = (
                    jnp.concatenate([found[k], found[many + k]], axis=0).astype(jnp.bfloat16)
                )

        def send(step, carry):
            c = lax.rem(step + me // (z.share * per_coarse), z.coarse)
            chunk = c * per_coarse + position
            for twin in range(z.share):
                device = chunk * z.share + twin

                @pl.when(device != me)
                def _():
                    parcel(chunk, device).start()

            return carry

        lax.fori_loop(0, z.coarse, send, 0)
    series[me] = outgoing[me // z.share]

    def receive(step, carry):
        source = lax.rem(me + step, z.devices)
        pltpu.make_async_remote_copy(
            src_ref=outgoing.at[0],
            dst_ref=series.at[source],
            send_sem=send_sem.at[source],
            recv_sem=recv_sem.at[source],
            device_id=at(source),
            device_id_type=MESH,
        ).wait_recv()
        return carry

    lax.fori_loop(1, z.devices, receive, 0)

    rows8 = z.frames_dev
    values = []
    for d in range(z.devices):
        both = series[d].astype(jnp.float32)
        values.append((both[:rows8], both[rows8:]))
    centred = []
    for k in range(2):
        total = values[0][k]
        for d in range(1, z.devices):
            total = total + values[d][k]
        mean = jnp.sum(total, axis=0, keepdims=True) * (1.0 / z.frames)
        part = [values[d][k] - mean for d in range(z.devices)]
        total = part[0] * part[0]
        for d in range(1, z.devices):
            total = total + part[d] * part[d]
        variance = jnp.sum(total, axis=0, keepdims=True) * (1.0 / z.frames)
        scale = 1.0 / jnp.sqrt(z.channels * (variance + EPSILON))
        centred.append((part, scale))
    wide = z.chunk // z.flat
    for d in range(z.devices):
        total = None
        for k in range(2):
            part, scale = centred[k]
            normed = part[d] * scale
            for lane in range(0, side, wide):
                piece = normed[:, lane : lane + wide]
                total = piece if total is None else total + piece
        turned[d * rows8 : (d + 1) * rows8, :] = total
    for span in range(z.spans):
        lanes = slice(span * LANES, (span + 1) * LANES)
        flat[:, lanes] = turned[lanes, :].T

    mine = pl.multiple_of(lax.rem(me, z.share) * z.block, TILE)
    tiles = [
        flat[pl.ds(pl.multiple_of(mine + TILE * k, TILE), TILE), :]
        for k in range(z.block // TILE)
    ]
    entry = 0
    row_in_tile = lax.broadcasted_iota(jnp.int32, (TILE, LANES), 0)
    for level in range(z.flat_levels + 1, z.local_levels + 1):
        width = z.width(level)
        merged = []
        for k in range(len(tiles)):
            h, g = upper_plan[entry], lower_plan[entry]
            entry += 1
            if width <= TILE:
                base = row_in_tile // width * width
                high, low = tiles[k], tiles[k]
                high_rows, low_rows = base + width // 2 + h, base + g
            else:
                many = width // TILE
                first = k // many * many + k % many // 2
                high, low = tiles[first + many // 2], tiles[first]
                high_rows, low_rows = h & (TILE - 1), g & (TILE - 1)
            merged.append(picked(high, high_rows) + later(picked(low, low_rows), h))
        tiles = merged
    for k, tile in enumerate(tiles):
        state[k] = tile

    def deliver(step, carry):
        device = lax.rem(me + step, z.devices)
        pltpu.make_async_remote_copy(
            src_ref=state.at[z.first_tile(device, z.local_levels)],
            dst_ref=tiles_in.at[me],
            send_sem=send2_sem.at[device],
            recv_sem=recv2_sem.at[me],
            device_id=at(device),
            device_id_type=MESH,
        ).start()
        return carry

    lax.fori_loop(1, z.devices, deliver, 0)
    tiles_in[me] = state[z.first_tile(me, z.local_levels)]

    def accept(step, carry):
        source = lax.rem(me + step, z.devices)
        pltpu.make_async_remote_copy(
            src_ref=state.at[0],
            dst_ref=tiles_in.at[source],
            send_sem=send2_sem.at[source],
            recv_sem=recv2_sem.at[source],
            device_id=at(source),
            device_id_type=MESH,
        ).wait_recv()
        return carry

    lax.fori_loop(1, z.devices, accept, 0)

    bands = [[tiles_in[d]] for d in range(z.devices)]
    for level in range(z.local_levels + 1, z.levels + 1):
        merged = []
        for band in range(len(bands) // 2):
            result = []
            for k in range(z.held[level]):
                h, g = upper_plan[entry], lower_plan[entry]
                entry += 1
                high = picked(bands[2 * band + 1][k // 2], h & (TILE - 1))
                low = picked(bands[2 * band][k // 2], g & (TILE - 1))
                result.append(high + later(low, h))
            merged.append(result)
        bands = merged
    for k, tile in enumerate(bands[0]):
        out_ref[k * TILE : (k + 1) * TILE, :] = tile

    @pl.when(me < z.devices - 1)
    def _():
        ahead.wait_send()

    def finish(step, carry):
        device = lax.rem(me + step, z.devices)
        pltpu.make_async_remote_copy(
            src_ref=outgoing.at[0],
            dst_ref=series.at[0],
            send_sem=send_sem.at[device],
            recv_sem=recv_sem.at[device],
            device_id=at(device),
            device_id_type=MESH,
        ).wait_send()
        pltpu.make_async_remote_copy(
            src_ref=state.at[0],
            dst_ref=tiles_in.at[0],
            send_sem=send2_sem.at[device],
            recv_sem=recv2_sem.at[device],
            device_id=at(device),
            device_id_type=MESH,
        ).wait_send()
        return carry

    lax.fori_loop(1, z.devices, finish, 0)


def per_device(axes, voltages, filter_taps, delay_plan):
    devices = lax.axis_size(axes[1]) * lax.axis_size(axes[2])
    z = Sizes(voltages, filter_taps, devices, lax.axis_size(axes[2]))
    table = jnp.asarray(dft_columns(z.length, z.chunk, z.flat))
    pieces = z.pieces(0)
    entries = sum(count for _, _, count in pieces)
    plan_rows = -(-2 * len(pieces) // LANES) * LANES
    f32, bf16, i32 = jnp.float32, jnp.bfloat16, jnp.int32
    vmem = pl.BlockSpec(memory_space=pltpu.VMEM)
    return pl.pallas_call(
        functools.partial(kernel, z, axes),
        out_shape=jax.ShapeDtypeStruct((z.block, z.frames), f32),
        in_specs=[pl.BlockSpec(memory_space=pl.ANY)] * 4,
        out_specs=vmem,
        scratch_shapes=[
            pltpu.VMEM((2, z.frames_dev, z.coarse, z.length), i32),
            pltpu.VMEM((z.frames_dev, 2 * z.coarse, z.length), bf16),
            pltpu.VMEM(filter_taps.shape, f32),
            pltpu.VMEM(delay_plan.shape, i32),
            pltpu.VMEM(table.shape, bf16),
            pltpu.VMEM((z.taps - 1, 2 * z.coarse, z.length), bf16),
            pltpu.VMEM((2 * z.frames_dev * z.coarse, z.length), bf16),
            pltpu.VMEM((z.chunk // LANES, z.frames_dev * z.coarse, LANES), f32),
            pltpu.VMEM((z.channels // z.chunk, 2 * z.frames_dev, z.chunk // 2), bf16),
            pltpu.VMEM((z.devices, 2 * z.frames_dev, z.chunk // 2), bf16),
            pltpu.VMEM((z.frames, z.chunk // z.flat), f32),
            pltpu.VMEM((z.chunk // z.flat, z.frames), f32),
            pltpu.VMEM((z.block // TILE, TILE, z.frames), f32),
            pltpu.VMEM((z.devices, TILE, z.frames), f32),
            pltpu.VMEM((plan_rows, LANES), i32),
            pltpu.VMEM((LANES, plan_rows), i32),
            pltpu.VMEM((entries, TILE, LANES), i32),
            pltpu.VMEM((entries, TILE, LANES), i32),
            pltpu.SemaphoreType.DMA((4,)),
            pltpu.SemaphoreType.DMA((table.shape[0],)),
            pltpu.SemaphoreType.DMA((2,)),
            pltpu.SemaphoreType.DMA((z.devices,)),
            pltpu.SemaphoreType.DMA((z.devices,)),
            pltpu.SemaphoreType.DMA((z.devices,)),
            pltpu.SemaphoreType.DMA((z.devices,)),
        ],
        compiler_params=pltpu.CompilerParams(
            collective_id=0, has_side_effects=True, vmem_limit_bytes=63 * 2**20
        ),
    )(voltages, filter_taps, delay_plan, table)


def solution(mesh):
    axes = ("beam", "freq", "section")
    placed = (P(axes, None, None, None), P(), P())
    return jax.shard_map(
        functools.partial(per_device, axes),
        mesh=mesh,
        in_specs=placed,
        out_specs=P(axes, None),
        check_vma=False,
    )
```

```python
import functools
import math

import jax
import jax.numpy as jnp
import numpy as np
from jax import lax
from jax.experimental import pallas as pl
from jax.experimental.pallas import tpu as pltpu
from jax.sharding import PartitionSpec as P

NDELAY = 2048

EPSILON = 1e-05

LANES = 128
TILE = 8
COLUMNS = 256
MESH = pl.DeviceIdType.MESH


def dft_columns(length, chunk, flat):
    wide = chunk // flat
    place = np.arange(length)
    channel = place // chunk * chunk + place % wide * flat + place % chunk // wide
    phase = np.arange(length)[:, None] * (channel[None, :] - length // 2) % length
    angle = phase.astype(np.float32) * np.float32(2.0 * math.pi / length)
    cosine = np.cos(angle).astype(jnp.bfloat16).reshape(length, -1, COLUMNS)
    sine = np.sin(angle).astype(jnp.bfloat16).reshape(length, -1, COLUMNS)
    return np.ascontiguousarray(np.concatenate([cosine, sine], axis=2).transpose(1, 0, 2))


class Sizes:
    def __init__(self, voltages, taps, devices, sections):
        self.devices, self.sections = devices, sections
        self.frames_dev, self.coarse, _, self.length = voltages.shape
        self.taps = taps.shape[0]
        self.channels = self.coarse * self.length
        self.frames = self.frames_dev * devices
        self.merges = devices.bit_length() - 1
        self.levels = self.channels.bit_length() - 1
        self.flat_levels = (self.channels // NDELAY).bit_length() - 1
        self.flat = 1 << self.flat_levels
        self.local_levels = self.levels - self.merges
        self.block = NDELAY // devices
        own = self.channels // devices
        self.chunk = max(own, LANES * self.flat)
        self.share = self.chunk // own
        self.spans = self.frames // LANES
        self.held = {self.levels: self.block // TILE}
        for level in range(self.levels, self.local_levels, -1):
            self.held[level - 1] = max(1, self.held[level] // 2)

    def width(self, level):
        return max(1, NDELAY * 2**level // self.channels)

    def offset(self, level):
        return sum((self.channels >> m) * self.width(m) for m in range(1, level))

    def first_tile(self, device, level):
        tile, held = device * self.held[self.levels], self.held[self.levels]
        for _ in range(self.levels - level):
            tile = tile // 2
        return tile

    def pieces(self, me):
        found = []
        for level in range(self.flat_levels + 1, self.local_levels + 1):
            found.append((level, self.offset(level) + me * self.block, self.block // TILE))
        for level in range(self.local_levels + 1, self.levels + 1):
            for band in range(self.channels >> level):
                start = self.offset(level) + band * self.width(level)
                found.append((level, start + TILE * self.first_tile(me, level), self.held[level]))
        return found


def picked(tile, rows):
    return jnp.concatenate(
        [
            jnp.take_along_axis(
                tile[:, at : at + LANES], rows, axis=0, mode="promise_in_bounds"
            )
            for at in range(0, tile.shape[1], LANES)
        ],
        axis=1,
    )


def later(tile, shift):
    place = lax.broadcasted_iota(jnp.int32, shift.shape, 1) + shift
    inside, span = place & (LANES - 1), place // LANES
    spans = tile.shape[1] // LANES
    turned = [
        jnp.take_along_axis(
            tile[:, s * LANES : (s + 1) * LANES], inside, axis=1, mode="promise_in_bounds"
        )
        for s in range(spans)
    ]
    result = []
    for out in range(spans):
        total = jnp.where(span == 0, turned[out], 0.0)
        for s in range(out + 1, spans):
            total = jnp.where(span == s - out, turned[s], total)
        result.append(total)
    return jnp.concatenate(result, axis=1)


def kernel(
    z,
    axes,
    x_hbm,
    taps_hbm,
    plan_hbm,
    table_ref,
    out_ref,
    raw,
    x_ref,
    taps_ref,
    plan_ref,
    table,
    halo,
    lhs,
    power,
    outgoing,
    series,
    turned,
    flat,
    state,
    tiles_in,
    plan_rows,
    plan_columns,
    upper_plan,
    lower_plan,
    load_sem,
    table_sem,
    halo_sem,
    send_sem,
    recv_sem,
    send2_sem,
    recv2_sem,
):
    beam = lax.axis_index(axes[0])
    me = lax.axis_index(axes[1]) * z.sections + lax.axis_index(axes[2])

    def at(device):
        return (beam, device // z.sections, lax.rem(device, z.sections))

    voltage_loads = [
        pltpu.make_async_copy(x_hbm.at[:, :, part], raw.at[part], load_sem.at[part])
        for part in range(2)
    ]
    plan_load = pltpu.make_async_copy(plan_hbm, plan_ref, load_sem.at[2])
    taps_load = pltpu.make_async_copy(taps_hbm, taps_ref, load_sem.at[3])
    for load in (*voltage_loads, plan_load, taps_load):
        load.start()
    loads = []
    for part in range(table_ref.shape[0]):
        loads.append(
            pltpu.make_async_copy(table_ref.at[part], table.at[part], table_sem.at[part])
        )
        loads[-1].start()

    barrier = pltpu.get_barrier_semaphore()

    def greet(step, carry):
        pl.semaphore_signal(
            barrier, inc=1, device_id=at(lax.rem(me + step, z.devices)), device_id_type=MESH
        )
        return carry

    lax.fori_loop(1, z.devices, greet, 0)
    for load in voltage_loads:
        load.wait()

    before = z.taps - 1
    ahead = []
    for piece in range(z.length // COLUMNS):
        lanes = pl.ds(piece * COLUMNS, COLUMNS)
        ahead.append(
            pltpu.make_async_remote_copy(
                src_ref=x_ref.at[pl.ds(z.frames_dev - before, before), :, lanes],
                dst_ref=halo.at[:, :, lanes],
                send_sem=halo_sem.at[0, piece],
                recv_sem=halo_sem.at[1, piece],
                device_id=at(lax.rem(me + 1, z.devices)),
                device_id_type=MESH,
            )
        )
    for piece, copy in enumerate(ahead):
        lanes = slice(piece * COLUMNS, (piece + 1) * COLUMNS)
        for n in range(z.frames_dev):
            both = jnp.concatenate([raw[0, n, :, lanes], raw[1, n, :, lanes]], axis=0)
            x_ref[n, :, lanes] = both.astype(jnp.float32).astype(jnp.bfloat16)
        if piece == 0:
            pl.semaphore_wait(barrier, z.devices - 1)

        @pl.when(me < z.devices - 1)
        def _():
            copy.start()

    @pl.when(me == 0)
    def _():
        halo[...] = jnp.zeros_like(halo)

    pieces = z.pieces(me)
    plan_load.wait()
    plan_rows[...] = jnp.zeros_like(plan_rows)
    for piece, (_, start, _) in enumerate(pieces):
        base = pl.multiple_of(start // LANES * LANES, LANES)
        plan_rows[2 * piece : 2 * piece + 2, :] = plan_ref[:, pl.ds(base, LANES)]
    for row in range(0, plan_rows.shape[0], LANES):
        plan_columns[:, row : row + LANES] = plan_rows[row : row + LANES, :].T
    entry = 0
    for piece, (_, start, count) in enumerate(pieces):
        for tile in range(count):
            row = pl.multiple_of(lax.rem(start, LANES) + TILE * tile, TILE)
            both = plan_columns[pl.ds(row, TILE), 2 * piece : 2 * piece + 2]
            upper_plan[entry] = jnp.broadcast_to(both[:, 0:1], (TILE, LANES))
            lower_plan[entry] = jnp.broadcast_to(both[:, 1:2], (TILE, LANES))
            entry += 1

    taps_load.wait()
    half = z.coarse
    rows = z.frames_dev * z.coarse
    for lane in range(0, z.length, LANES):
        lanes = slice(lane, lane + LANES)
        if lane % COLUMNS == 0:

            @pl.when(me > 0)
            def _():
                ahead[lane // COLUMNS].wait_recv()

        window = [halo[n, :, lanes].astype(jnp.float32) for n in range(before)]
        window += [x_ref[n, :, lanes].astype(jnp.float32) for n in range(z.frames_dev)]
        taps = [taps_ref[j : j + 1, lanes] for j in range(z.taps)]
        summed = []
        for n in range(z.frames_dev):
            total = window[n] * taps[0]
            for j in range(1, z.taps):
                total = total + window[n + j] * taps[j]
            summed.append(total)
        for part in range(2):
            for n in range(0, z.frames_dev, 2):
                own = slice(part * half, (part + 1) * half)
                pair = jnp.concatenate([summed[n][own], summed[n + 1][own]], axis=0)
                first = part * rows + n * half
                lhs[first : first + 2 * half, lanes] = pair.astype(jnp.bfloat16)

    per_coarse = z.length // z.chunk
    parts = z.chunk // COLUMNS
    side = z.chunk // 2

    def parcel(chunk, device):
        return pltpu.make_async_remote_copy(
            src_ref=outgoing.at[chunk],
            dst_ref=series.at[me],
            send_sem=send_sem.at[device],
            recv_sem=recv_sem.at[me],
            device_id=at(device),
            device_id_type=MESH,
        )

    for position in range(per_coarse):
        for part in range(parts):
            index = position * parts + part
            loads[index].wait()
            product = jnp.dot(lhs[...], table[index], preferred_element_type=jnp.float32)
            real = product[:rows, :COLUMNS] + product[rows:, COLUMNS:]
            imag = product[rows:, :COLUMNS] - product[:rows, COLUMNS:]
            squared = real * real + imag * imag
            for lane in range(0, COLUMNS, LANES):
                power[(part * COLUMNS + lane) // LANES] = squared[:, lane : lane + LANES]
        for c in range(z.coarse):
            found = [
                power[k, pl.ds(c, z.frames_dev, stride=z.coarse), :]
                for k in range(z.chunk // LANES)
            ]
            many = len(found) // 2
            for k in range(many):
                outgoing[c * per_coarse + position, :, k * LANES : (k + 1) * LANES] = (
                    jnp.concatenate([found[k], found[many + k]], axis=0).astype(jnp.bfloat16)
                )

        def send(step, carry):
            c = lax.rem(step + me // (z.share * per_coarse), z.coarse)
            chunk = c * per_coarse + position
            for twin in range(z.share):
                device = chunk * z.share + twin

                @pl.when(device != me)
                def _():
                    parcel(chunk, device).start()

            return carry

        lax.fori_loop(0, z.coarse, send, 0)
    series[me] = outgoing[me // z.share]

    def receive(step, carry):
        source = lax.rem(me + step, z.devices)
        pltpu.make_async_remote_copy(
            src_ref=outgoing.at[0],
            dst_ref=series.at[source],
            send_sem=send_sem.at[source],
            recv_sem=recv_sem.at[source],
            device_id=at(source),
            device_id_type=MESH,
        ).wait_recv()
        return carry

    lax.fori_loop(1, z.devices, receive, 0)

    rows8 = z.frames_dev
    values = []
    for d in range(z.devices):
        both = series[d].astype(jnp.float32)
        values.append((both[:rows8], both[rows8:]))
    centred = []
    for k in range(2):
        total = values[0][k]
        for d in range(1, z.devices):
            total = total + values[d][k]
        mean = jnp.sum(total, axis=0, keepdims=True) * (1.0 / z.frames)
        part = [values[d][k] - mean for d in range(z.devices)]
        total = part[0] * part[0]
        for d in range(1, z.devices):
            total = total + part[d] * part[d]
        variance = jnp.sum(total, axis=0, keepdims=True) * (1.0 / z.frames)
        scale = 1.0 / jnp.sqrt(z.channels * (variance + EPSILON))
        centred.append((part, scale))
    wide = z.chunk // z.flat
    for d in range(z.devices):
        total = None
        for k in range(2):
            part, scale = centred[k]
            normed = part[d] * scale
            for lane in range(0, side, wide):
                piece = normed[:, lane : lane + wide]
                total = piece if total is None else total + piece
        turned[d * rows8 : (d + 1) * rows8, :] = total
    for span in range(z.spans):
        lanes = slice(span * LANES, (span + 1) * LANES)
        flat[:, lanes] = turned[lanes, :].T

    mine = pl.multiple_of(lax.rem(me, z.share) * z.block, TILE)
    tiles = [
        flat[pl.ds(pl.multiple_of(mine + TILE * k, TILE), TILE), :]
        for k in range(z.block // TILE)
    ]
    entry = 0
    row_in_tile = lax.broadcasted_iota(jnp.int32, (TILE, LANES), 0)
    for level in range(z.flat_levels + 1, z.local_levels + 1):
        width = z.width(level)
        merged = []
        for k in range(len(tiles)):
            h, g = upper_plan[entry], lower_plan[entry]
            entry += 1
            if width <= TILE:
                base = row_in_tile // width * width
                high, low = tiles[k], tiles[k]
                high_rows, low_rows = base + width // 2 + h, base + g
            else:
                many = width // TILE
                first = k // many * many + k % many // 2
                high, low = tiles[first + many // 2], tiles[first]
                high_rows, low_rows = h & (TILE - 1), g & (TILE - 1)
            merged.append(picked(high, high_rows) + later(picked(low, low_rows), h))
        tiles = merged
    for k, tile in enumerate(tiles):
        state[k] = tile

    def deliver(step, carry):
        device = lax.rem(me + step, z.devices)
        pltpu.make_async_remote_copy(
            src_ref=state.at[z.first_tile(device, z.local_levels)],
            dst_ref=tiles_in.at[me],
            send_sem=send2_sem.at[device],
            recv_sem=recv2_sem.at[me],
            device_id=at(device),
            device_id_type=MESH,
        ).start()
        return carry

    lax.fori_loop(1, z.devices, deliver, 0)
    tiles_in[me] = state[z.first_tile(me, z.local_levels)]

    def accept(step, carry):
        source = lax.rem(me + step, z.devices)
        pltpu.make_async_remote_copy(
            src_ref=state.at[0],
            dst_ref=tiles_in.at[source],
            send_sem=send2_sem.at[source],
            recv_sem=recv2_sem.at[source],
            device_id=at(source),
            device_id_type=MESH,
        ).wait_recv()
        return carry

    lax.fori_loop(1, z.devices, accept, 0)

    bands = [[tiles_in[d]] for d in range(z.devices)]
    for level in range(z.local_levels + 1, z.levels + 1):
        merged = []
        for band in range(len(bands) // 2):
            result = []
            for k in range(z.held[level]):
                h, g = upper_plan[entry], lower_plan[entry]
                entry += 1
                high = picked(bands[2 * band + 1][k // 2], h & (TILE - 1))
                low = picked(bands[2 * band][k // 2], g & (TILE - 1))
                result.append(high + later(low, h))
            merged.append(result)
        bands = merged
    for k, tile in enumerate(bands[0]):
        out_ref[k * TILE : (k + 1) * TILE, :] = tile

    @pl.when(me < z.devices - 1)
    def _():
        for copy in ahead:
            copy.wait_send()

    def finish(step, carry):
        device = lax.rem(me + step, z.devices)
        pltpu.make_async_remote_copy(
            src_ref=outgoing.at[0],
            dst_ref=series.at[0],
            send_sem=send_sem.at[device],
            recv_sem=recv_sem.at[device],
            device_id=at(device),
            device_id_type=MESH,
        ).wait_send()
        pltpu.make_async_remote_copy(
            src_ref=state.at[0],
            dst_ref=tiles_in.at[0],
            send_sem=send2_sem.at[device],
            recv_sem=recv2_sem.at[device],
            device_id=at(device),
            device_id_type=MESH,
        ).wait_send()
        return carry

    lax.fori_loop(1, z.devices, finish, 0)


def per_device(axes, voltages, filter_taps, delay_plan):
    devices = lax.axis_size(axes[1]) * lax.axis_size(axes[2])
    z = Sizes(voltages, filter_taps, devices, lax.axis_size(axes[2]))
    table = jnp.asarray(dft_columns(z.length, z.chunk, z.flat))
    pieces = z.pieces(0)
    entries = sum(count for _, _, count in pieces)
    plan_rows = -(-2 * len(pieces) // LANES) * LANES
    f32, bf16, i32 = jnp.float32, jnp.bfloat16, jnp.int32
    vmem = pl.BlockSpec(memory_space=pltpu.VMEM)
    return pl.pallas_call(
        functools.partial(kernel, z, axes),
        out_shape=jax.ShapeDtypeStruct((z.block, z.frames), f32),
        in_specs=[pl.BlockSpec(memory_space=pl.ANY)] * 4,
        out_specs=vmem,
        scratch_shapes=[
            pltpu.VMEM((2, z.frames_dev, z.coarse, z.length), i32),
            pltpu.VMEM((z.frames_dev, 2 * z.coarse, z.length), bf16),
            pltpu.VMEM(filter_taps.shape, f32),
            pltpu.VMEM(delay_plan.shape, i32),
            pltpu.VMEM(table.shape, bf16),
            pltpu.VMEM((z.taps - 1, 2 * z.coarse, z.length), bf16),
            pltpu.VMEM((2 * z.frames_dev * z.coarse, z.length), bf16),
            pltpu.VMEM((z.chunk // LANES, z.frames_dev * z.coarse, LANES), f32),
            pltpu.VMEM((z.channels // z.chunk, 2 * z.frames_dev, z.chunk // 2), bf16),
            pltpu.VMEM((z.devices, 2 * z.frames_dev, z.chunk // 2), bf16),
            pltpu.VMEM((z.frames, z.chunk // z.flat), f32),
            pltpu.VMEM((z.chunk // z.flat, z.frames), f32),
            pltpu.VMEM((z.block // TILE, TILE, z.frames), f32),
            pltpu.VMEM((z.devices, TILE, z.frames), f32),
            pltpu.VMEM((plan_rows, LANES), i32),
            pltpu.VMEM((LANES, plan_rows), i32),
            pltpu.VMEM((entries, TILE, LANES), i32),
            pltpu.VMEM((entries, TILE, LANES), i32),
            pltpu.SemaphoreType.DMA((4,)),
            pltpu.SemaphoreType.DMA((table.shape[0],)),
            pltpu.SemaphoreType.DMA((2, z.length // COLUMNS)),
            pltpu.SemaphoreType.DMA((z.devices,)),
            pltpu.SemaphoreType.DMA((z.devices,)),
            pltpu.SemaphoreType.DMA((z.devices,)),
            pltpu.SemaphoreType.DMA((z.devices,)),
        ],
        compiler_params=pltpu.CompilerParams(
            collective_id=0, has_side_effects=True, vmem_limit_bytes=63 * 2**20
        ),
    )(voltages, filter_taps, delay_plan, table)


def solution(mesh):
    axes = ("beam", "freq", "section")
    placed = (P(axes, None, None, None), P(), P())
    return jax.shard_map(
        functools.partial(per_device, axes),
        mesh=mesh,
        in_specs=placed,
        out_specs=P(axes, None),
        check_vma=False,
    )
```

```python
import functools
import math

import jax
import jax.numpy as jnp
import numpy as np
from jax import lax
from jax.experimental import pallas as pl
from jax.experimental.pallas import tpu as pltpu
from jax.sharding import PartitionSpec as P

NDELAY = 2048

EPSILON = 1e-05

LANES = 128
TILE = 8
COLUMNS = 256
MESH = pl.DeviceIdType.MESH


def dft_columns(length, chunk, flat):
    wide = chunk // flat
    place = np.arange(length)
    channel = place // chunk * chunk + place % wide * flat + place % chunk // wide
    phase = np.arange(length)[:, None] * (channel[None, :] - length // 2) % length
    angle = phase.astype(np.float32) * np.float32(2.0 * math.pi / length)
    cosine = np.cos(angle).astype(jnp.bfloat16).reshape(length, -1, COLUMNS)
    sine = np.sin(angle).astype(jnp.bfloat16).reshape(length, -1, COLUMNS)
    return np.ascontiguousarray(np.concatenate([cosine, sine], axis=2).transpose(1, 0, 2))


class Sizes:
    def __init__(self, voltages, taps, devices, sections):
        self.devices, self.sections = devices, sections
        self.frames_dev, self.coarse, _, self.length = voltages.shape
        self.taps = taps.shape[0]
        self.channels = self.coarse * self.length
        self.frames = self.frames_dev * devices
        self.merges = devices.bit_length() - 1
        self.levels = self.channels.bit_length() - 1
        self.flat_levels = (self.channels // NDELAY).bit_length() - 1
        self.flat = 1 << self.flat_levels
        self.local_levels = self.levels - self.merges
        self.block = NDELAY // devices
        own = self.channels // devices
        self.chunk = max(own, LANES * self.flat)
        self.share = self.chunk // own
        self.spans = self.frames // LANES
        self.held = {self.levels: self.block // TILE}
        for level in range(self.levels, self.local_levels, -1):
            self.held[level - 1] = max(1, self.held[level] // 2)

    def width(self, level):
        return max(1, NDELAY * 2**level // self.channels)

    def offset(self, level):
        return sum((self.channels >> m) * self.width(m) for m in range(1, level))

    def first_tile(self, device, level):
        tile, held = device * self.held[self.levels], self.held[self.levels]
        for _ in range(self.levels - level):
            tile = tile // 2
        return tile

    def pieces(self, me):
        found = []
        for level in range(self.flat_levels + 1, self.local_levels + 1):
            found.append((level, self.offset(level) + me * self.block, self.block // TILE))
        for level in range(self.local_levels + 1, self.levels + 1):
            for band in range(self.channels >> level):
                start = self.offset(level) + band * self.width(level)
                found.append((level, start + TILE * self.first_tile(me, level), self.held[level]))
        return found


def picked(tile, rows):
    return jnp.concatenate(
        [
            jnp.take_along_axis(
                tile[:, at : at + LANES], rows, axis=0, mode="promise_in_bounds"
            )
            for at in range(0, tile.shape[1], LANES)
        ],
        axis=1,
    )


def later(tile, shift):
    place = lax.broadcasted_iota(jnp.int32, shift.shape, 1) + shift
    inside, span = place & (LANES - 1), place // LANES
    spans = tile.shape[1] // LANES
    turned = [
        jnp.take_along_axis(
            tile[:, s * LANES : (s + 1) * LANES], inside, axis=1, mode="promise_in_bounds"
        )
        for s in range(spans)
    ]
    result = []
    for out in range(spans):
        total = jnp.where(span == 0, turned[out], 0.0)
        for s in range(out + 1, spans):
            total = jnp.where(span == s - out, turned[s], total)
        result.append(total)
    return jnp.concatenate(result, axis=1)


def kernel(
    z,
    axes,
    x_hbm,
    taps_hbm,
    plan_hbm,
    table_ref,
    out_ref,
    raw,
    x_ref,
    taps_ref,
    plan_ref,
    table,
    halo,
    lhs,
    power,
    outgoing,
    series,
    turned,
    flat,
    state,
    tiles_in,
    plan_rows,
    plan_columns,
    upper_plan,
    lower_plan,
    load_sem,
    table_sem,
    halo_sem,
    send_sem,
    recv_sem,
    send2_sem,
    recv2_sem,
):
    beam = lax.axis_index(axes[0])
    me = lax.axis_index(axes[1]) * z.sections + lax.axis_index(axes[2])

    def at(device):
        return (beam, device // z.sections, lax.rem(device, z.sections))

    voltage_loads = [
        pltpu.make_async_copy(x_hbm.at[:, :, part], raw.at[part], load_sem.at[part])
        for part in range(2)
    ]
    plan_load = pltpu.make_async_copy(plan_hbm, plan_ref, load_sem.at[2])
    taps_load = pltpu.make_async_copy(taps_hbm, taps_ref, load_sem.at[3])
    for load in (*voltage_loads, plan_load, taps_load):
        load.start()
    loads = []
    for part in range(table_ref.shape[0]):
        loads.append(
            pltpu.make_async_copy(table_ref.at[part], table.at[part], table_sem.at[part])
        )
        loads[-1].start()

    barrier = pltpu.get_barrier_semaphore()

    def greet(step, carry):
        pl.semaphore_signal(
            barrier, inc=1, device_id=at(lax.rem(me + step, z.devices)), device_id_type=MESH
        )
        return carry

    lax.fori_loop(1, z.devices, greet, 0)
    for load in voltage_loads:
        load.wait()

    before = z.taps - 1
    ahead = []
    for piece in range(z.length // COLUMNS):
        lanes = pl.ds(piece * COLUMNS, COLUMNS)
        ahead.append(
            pltpu.make_async_remote_copy(
                src_ref=x_ref.at[pl.ds(z.frames_dev - before, before), :, lanes],
                dst_ref=halo.at[:, :, lanes],
                send_sem=halo_sem.at[0, piece],
                recv_sem=halo_sem.at[1, piece],
                device_id=at(lax.rem(me + 1, z.devices)),
                device_id_type=MESH,
            )
        )
    for piece, copy in enumerate(ahead):
        lanes = slice(piece * COLUMNS, (piece + 1) * COLUMNS)
        for n in range(z.frames_dev):
            both = jnp.concatenate([raw[0, n, :, lanes], raw[1, n, :, lanes]], axis=0)
            x_ref[n, :, lanes] = both.astype(jnp.float32).astype(jnp.bfloat16)
        if piece == 0:
            pl.semaphore_wait(barrier, z.devices - 1)

        @pl.when(me < z.devices - 1)
        def _():
            copy.start()

    @pl.when(me == 0)
    def _():
        halo[...] = jnp.zeros_like(halo)

    pieces = z.pieces(me)
    plan_load.wait()
    plan_rows[...] = jnp.zeros_like(plan_rows)
    for piece, (_, start, _) in enumerate(pieces):
        base = pl.multiple_of(start // LANES * LANES, LANES)
        plan_rows[2 * piece : 2 * piece + 2, :] = plan_ref[:, pl.ds(base, LANES)]
    for row in range(0, plan_rows.shape[0], LANES):
        plan_columns[:, row : row + LANES] = plan_rows[row : row + LANES, :].T
    entry = 0
    for piece, (_, start, count) in enumerate(pieces):
        for tile in range(count):
            row = pl.multiple_of(lax.rem(start, LANES) + TILE * tile, TILE)
            both = plan_columns[pl.ds(row, TILE), 2 * piece : 2 * piece + 2]
            upper_plan[entry] = jnp.broadcast_to(both[:, 0:1], (TILE, LANES))
            lower_plan[entry] = jnp.broadcast_to(both[:, 1:2], (TILE, LANES))
            entry += 1

    taps_load.wait()
    half = z.coarse
    rows = z.frames_dev * z.coarse
    for lane in range(0, z.length, LANES):
        lanes = slice(lane, lane + LANES)
        if lane % COLUMNS == 0:

            @pl.when(me > 0)
            def _():
                ahead[lane // COLUMNS].wait_recv()

        window = [halo[n, :, lanes].astype(jnp.float32) for n in range(before)]
        window += [x_ref[n, :, lanes].astype(jnp.float32) for n in range(z.frames_dev)]
        taps = [taps_ref[j : j + 1, lanes] for j in range(z.taps)]
        summed = []
        for n in range(z.frames_dev):
            total = window[n] * taps[0]
            for j in range(1, z.taps):
                total = total + window[n + j] * taps[j]
            summed.append(total)
        for part in range(2):
            for n in range(0, z.frames_dev, 2):
                own = slice(part * half, (part + 1) * half)
                pair = jnp.concatenate([summed[n][own], summed[n + 1][own]], axis=0)
                first = part * rows + n * half
                lhs[first : first + 2 * half, lanes] = pair.astype(jnp.bfloat16)

    per_coarse = z.length // z.chunk
    parts = z.chunk // COLUMNS
    side = z.chunk // 2

    def parcel(chunk, device):
        return pltpu.make_async_remote_copy(
            src_ref=outgoing.at[chunk],
            dst_ref=series.at[me],
            send_sem=send_sem.at[device],
            recv_sem=recv_sem.at[me],
            device_id=at(device),
            device_id_type=MESH,
        )

    for position in range(per_coarse):
        for part in range(parts):
            index = position * parts + part
            loads[index].wait()
            product = jnp.dot(lhs[...], table[index], preferred_element_type=jnp.float32)
            real = product[:rows, :COLUMNS] + product[rows:, COLUMNS:]
            imag = product[rows:, :COLUMNS] - product[:rows, COLUMNS:]
            squared = real * real + imag * imag
            for lane in range(0, COLUMNS, LANES):
                power[(part * COLUMNS + lane) // LANES] = squared[:, lane : lane + LANES]
        for c in range(z.coarse):
            found = [
                power[k, pl.ds(c, z.frames_dev, stride=z.coarse), :]
                for k in range(z.chunk // LANES)
            ]
            many = len(found) // 2
            for k in range(many):
                outgoing[c * per_coarse + position, :, k * LANES : (k + 1) * LANES] = (
                    jnp.concatenate([found[k], found[many + k]], axis=0).astype(jnp.bfloat16)
                )

        def send(step, carry):
            c = lax.rem(step + z.coarse // 2 + me // (z.share * per_coarse), z.coarse)
            chunk = c * per_coarse + position
            for twin in range(z.share):
                device = chunk * z.share + twin

                @pl.when(device != me)
                def _():
                    parcel(chunk, device).start()

            return carry

        lax.fori_loop(0, z.coarse, send, 0)
    series[me] = outgoing[me // z.share]

    def receive(step, carry):
        source = lax.rem(me + step, z.devices)
        pltpu.make_async_remote_copy(
            src_ref=outgoing.at[0],
            dst_ref=series.at[source],
            send_sem=send_sem.at[source],
            recv_sem=recv_sem.at[source],
            device_id=at(source),
            device_id_type=MESH,
        ).wait_recv()
        return carry

    lax.fori_loop(1, z.devices, receive, 0)

    rows8 = z.frames_dev
    values = []
    for d in range(z.devices):
        both = series[d].astype(jnp.float32)
        values.append((both[:rows8], both[rows8:]))
    centred = []
    for k in range(2):
        total = values[0][k]
        for d in range(1, z.devices):
            total = total + values[d][k]
        mean = jnp.sum(total, axis=0, keepdims=True) * (1.0 / z.frames)
        part = [values[d][k] - mean for d in range(z.devices)]
        total = part[0] * part[0]
        for d in range(1, z.devices):
            total = total + part[d] * part[d]
        variance = jnp.sum(total, axis=0, keepdims=True) * (1.0 / z.frames)
        scale = 1.0 / jnp.sqrt(z.channels * (variance + EPSILON))
        centred.append((part, scale))
    wide = z.chunk // z.flat
    for d in range(z.devices):
        total = None
        for k in range(2):
            part, scale = centred[k]
            normed = part[d] * scale
            for lane in range(0, side, wide):
                piece = normed[:, lane : lane + wide]
                total = piece if total is None else total + piece
        turned[d * rows8 : (d + 1) * rows8, :] = total
    for span in range(z.spans):
        lanes = slice(span * LANES, (span + 1) * LANES)
        flat[:, lanes] = turned[lanes, :].T

    mine = pl.multiple_of(lax.rem(me, z.share) * z.block, TILE)
    tiles = [
        flat[pl.ds(pl.multiple_of(mine + TILE * k, TILE), TILE), :]
        for k in range(z.block // TILE)
    ]
    entry = 0
    row_in_tile = lax.broadcasted_iota(jnp.int32, (TILE, LANES), 0)
    for level in range(z.flat_levels + 1, z.local_levels + 1):
        width = z.width(level)
        merged = []
        for k in range(len(tiles)):
            h, g = upper_plan[entry], lower_plan[entry]
            entry += 1
            if width <= TILE:
                base = row_in_tile // width * width
                high, low = tiles[k], tiles[k]
                high_rows, low_rows = base + width // 2 + h, base + g
            else:
                many = width // TILE
                first = k // many * many + k % many // 2
                high, low = tiles[first + many // 2], tiles[first]
                high_rows, low_rows = h & (TILE - 1), g & (TILE - 1)
            merged.append(picked(high, high_rows) + later(picked(low, low_rows), h))
        tiles = merged
    for k, tile in enumerate(tiles):
        state[k] = tile

    def deliver(step, carry):
        far = (step + 1) // 2 * (1 - 2 * lax.rem(step, 2))
        device = lax.rem(me + z.devices // 2 + far + z.devices, z.devices)
        pltpu.make_async_remote_copy(
            src_ref=state.at[z.first_tile(device, z.local_levels)],
            dst_ref=tiles_in.at[me],
            send_sem=send2_sem.at[device],
            recv_sem=recv2_sem.at[me],
            device_id=at(device),
            device_id_type=MESH,
        ).start()
        return carry

    lax.fori_loop(0, z.devices - 1, deliver, 0)
    tiles_in[me] = state[z.first_tile(me, z.local_levels)]

    def accept(step, carry):
        source = lax.rem(me + step, z.devices)
        pltpu.make_async_remote_copy(
            src_ref=state.at[0],
            dst_ref=tiles_in.at[source],
            send_sem=send2_sem.at[source],
            recv_sem=recv2_sem.at[source],
            device_id=at(source),
            device_id_type=MESH,
        ).wait_recv()
        return carry

    lax.fori_loop(1, z.devices, accept, 0)

    bands = [[tiles_in[d]] for d in range(z.devices)]
    for level in range(z.local_levels + 1, z.levels + 1):
        merged = []
        for band in range(len(bands) // 2):
            result = []
            for k in range(z.held[level]):
                h, g = upper_plan[entry], lower_plan[entry]
                entry += 1
                high = picked(bands[2 * band + 1][k // 2], h & (TILE - 1))
                low = picked(bands[2 * band][k // 2], g & (TILE - 1))
                result.append(high + later(low, h))
            merged.append(result)
        bands = merged
    for k, tile in enumerate(bands[0]):
        out_ref[k * TILE : (k + 1) * TILE, :] = tile

    @pl.when(me < z.devices - 1)
    def _():
        for copy in ahead:
            copy.wait_send()

    def finish(step, carry):
        device = lax.rem(me + step, z.devices)
        pltpu.make_async_remote_copy(
            src_ref=outgoing.at[0],
            dst_ref=series.at[0],
            send_sem=send_sem.at[device],
            recv_sem=recv_sem.at[device],
            device_id=at(device),
            device_id_type=MESH,
        ).wait_send()
        pltpu.make_async_remote_copy(
            src_ref=state.at[0],
            dst_ref=tiles_in.at[0],
            send_sem=send2_sem.at[device],
            recv_sem=recv2_sem.at[device],
            device_id=at(device),
            device_id_type=MESH,
        ).wait_send()
        return carry

    lax.fori_loop(1, z.devices, finish, 0)


def per_device(axes, voltages, filter_taps, delay_plan):
    devices = lax.axis_size(axes[1]) * lax.axis_size(axes[2])
    z = Sizes(voltages, filter_taps, devices, lax.axis_size(axes[2]))
    table = jnp.asarray(dft_columns(z.length, z.chunk, z.flat))
    pieces = z.pieces(0)
    entries = sum(count for _, _, count in pieces)
    plan_rows = -(-2 * len(pieces) // LANES) * LANES
    f32, bf16, i32 = jnp.float32, jnp.bfloat16, jnp.int32
    vmem = pl.BlockSpec(memory_space=pltpu.VMEM)
    return pl.pallas_call(
        functools.partial(kernel, z, axes),
        out_shape=jax.ShapeDtypeStruct((z.block, z.frames), f32),
        in_specs=[pl.BlockSpec(memory_space=pl.ANY)] * 4,
        out_specs=vmem,
        scratch_shapes=[
            pltpu.VMEM((2, z.frames_dev, z.coarse, z.length), i32),
            pltpu.VMEM((z.frames_dev, 2 * z.coarse, z.length), bf16),
            pltpu.VMEM(filter_taps.shape, f32),
            pltpu.VMEM(delay_plan.shape, i32),
            pltpu.VMEM(table.shape, bf16),
            pltpu.VMEM((z.taps - 1, 2 * z.coarse, z.length), bf16),
            pltpu.VMEM((2 * z.frames_dev * z.coarse, z.length), bf16),
            pltpu.VMEM((z.chunk // LANES, z.frames_dev * z.coarse, LANES), f32),
            pltpu.VMEM((z.channels // z.chunk, 2 * z.frames_dev, z.chunk // 2), bf16),
            pltpu.VMEM((z.devices, 2 * z.frames_dev, z.chunk // 2), bf16),
            pltpu.VMEM((z.frames, z.chunk // z.flat), f32),
            pltpu.VMEM((z.chunk // z.flat, z.frames), f32),
            pltpu.VMEM((z.block // TILE, TILE, z.frames), f32),
            pltpu.VMEM((z.devices, TILE, z.frames), f32),
            pltpu.VMEM((plan_rows, LANES), i32),
            pltpu.VMEM((LANES, plan_rows), i32),
            pltpu.VMEM((entries, TILE, LANES), i32),
            pltpu.VMEM((entries, TILE, LANES), i32),
            pltpu.SemaphoreType.DMA((4,)),
            pltpu.SemaphoreType.DMA((table.shape[0],)),
            pltpu.SemaphoreType.DMA((2, z.length // COLUMNS)),
            pltpu.SemaphoreType.DMA((z.devices,)),
            pltpu.SemaphoreType.DMA((z.devices,)),
            pltpu.SemaphoreType.DMA((z.devices,)),
            pltpu.SemaphoreType.DMA((z.devices,)),
        ],
        compiler_params=pltpu.CompilerParams(
            collective_id=0, has_side_effects=True, vmem_limit_bytes=63 * 2**20
        ),
    )(voltages, filter_taps, delay_plan, table)


def solution(mesh):
    axes = ("beam", "freq", "section")
    placed = (P(axes, None, None, None), P(), P())
    return jax.shard_map(
        functools.partial(per_device, axes),
        mesh=mesh,
        in_specs=placed,
        out_specs=P(axes, None),
        check_vma=False,
    )
```
